32 devices in a mesh: hi: 4 (over y, core), lo: 8 (over z, x).
Axes of the slice: x: 2, y: 2, z: 4, core: 2. Of those that a mesh axis runs over, the one named last changes fastest.
Arguments:
- panel: float32 [262144, 128], P(('hi', 'lo')), may hold values from -6 to 6
- row_signs: float32 [262144, 1], P(('hi', 'lo')), may hold values from -4 to 4
- sample_rows: int32 [1024], replicated, may hold values from 0 to 262143, as said below
Outputs:
- sketch: float32 [1024, 128], P(('hi', 'lo'))
The draws below stay inside these ranges and needn't reach their ends.
Inputs may be any that keep to these rules, and one draw needn't show every extreme that they name: `sample_rows`: repeats may occur; they fall very unevenly on the devices that hold the rows.
All inputs are finite; a program needn't handle non-finite values.
Results may differ from the reference program's by a relative error of at most 0.000098.
Values sent between devices are 32-bit elements; how exact they have to be, the bound alone decides.
A program may use at most 64 MiB of HBM per device.

```python
import jax
import jax.numpy as jnp

ROWS_DEV = 8192
COLS = 128
ROWS = 262144
SAMPLE = 1024
N_HI = 4
N_LO = 8


def draw_sample_rows(key, part):
    first_key, second_key = jax.random.split(jax.random.fold_in(key, 11))
    ndev = N_HI * N_LO
    picks = jax.random.randint(first_key, (SAMPLE,), 0, ndev)
    owner = (picks * picks + picks) // ndev
    within = jax.random.randint(second_key, (SAMPLE,), 0, ROWS_DEV)
    rows = (owner * ROWS_DEV + within).astype(jnp.int32)
    rows = rows.at[0].set(jnp.int32(0))
    rows = rows.at[SAMPLE - 1].set(jnp.int32(ROWS - 1))
    return rows


def levels(rng, extent, shards, least, high):
    gain = 1.0
    for dim, shards_of in shards:
        draws = jax.random.uniform(jax.random.fold_in(jax.random.fold_in(rng, 6), dim), (shards_of,), jnp.float32, least / len(shards), high / len(shards))
        gain = gain * jnp.repeat(jnp.exp(draws), extent[dim] // shards_of).reshape((-1,) + (1,) * (len(extent) - 1 - dim))
    return gain


def bell_draw(key, dims, spread, reach, cuts=(), held_as=jnp.bfloat16):
    drawn = spread * jax.random.normal(key, dims, jnp.float32)
    if cuts:
        drawn = drawn * levels(key, dims, cuts, -0.22, 0.18)
    return jnp.clip(drawn, -reach, reach).astype(held_as)


def setup_inputs(seed: int = 0) -> dict:
    seeds = jax.random.split(jax.random.key(seed), 4)
    panel = bell_draw(seeds[0], (ROWS, COLS), 1.0, 6.0, ((0, 32),), jnp.float32)
    row_signs = bell_draw(seeds[1], (ROWS, 1), 1.0, 4.0, ((0, 32),), jnp.float32)
    sample_rows = draw_sample_rows(jax.random.fold_in(seeds[3], 71), 0)
    return {"panel": panel, "row_signs": row_signs, "sample_rows": sample_rows}


def reference(panel, row_signs, sample_rows):
    total = panel.shape[0]
    width = panel.shape[1]
    field = row_signs * panel
    half = 1
    while half < total:
        shaped = field.reshape(total // (2 * half), 2, half, width)
        first = shaped[:, 0]
        second = shaped[:, 1]
        field = jnp.stack([first + second, first - second], axis=1).reshape(total, width)
        half = half * 2
    picked = jnp.take(field, sample_rows, axis=0)
    return picked / jnp.sqrt(jnp.float32(total))
```

```python
import jax
import jax.numpy as jnp
from jax import lax
from jax.sharding import PartitionSpec as P


def hadamard(order):
    left = jnp.arange(order, dtype=jnp.int32)[:, None]
    right = jnp.arange(order, dtype=jnp.int32)[None, :]
    parity = lax.population_count(left & right) & 1
    return (1 - 2 * parity).astype(jnp.float32)


def local_transform(field):
    count, width = field.shape
    inner = min(count, 128)
    outer = count // inner
    shaped = field.reshape(outer, inner, width)
    step_one = jnp.einsum("eb,abk->aek", hadamard(inner), shaped, precision=lax.Precision.HIGHEST)
    step_two = jnp.einsum("ca,aek->cek", hadamard(outer), step_one, precision=lax.Precision.HIGHEST)
    return step_two.reshape(count, width)


def body(panel, row_signs, sample_rows):
    count, width = panel.shape
    devices = lax.axis_size("hi") * lax.axis_size("lo")
    device_id = lax.axis_index("hi") * lax.axis_size("lo") + lax.axis_index("lo")
    field = local_transform(row_signs * panel)
    rows = jnp.take(field, sample_rows % count, axis=0)
    parity = lax.population_count((sample_rows // count) & device_id) & 1
    sign = (1 - 2 * parity).astype(jnp.float32) / jnp.sqrt(jnp.float32(count * devices))
    return lax.psum_scatter(sign[:, None] * rows, ("hi", "lo"), scatter_dimension=0, tiled=True)


def solution(mesh):
    placed = (P(("hi", "lo"), None), P(("hi", "lo"), None), P())
    return jax.shard_map(
        body, mesh=mesh, in_specs=placed, out_specs=P(("hi", "lo"), None), check_vma=False
    )
```

```python
import functools
import math

import jax
import jax.numpy as jnp
from jax import lax
from jax.experimental import pallas as pl
from jax.experimental.pallas import tpu as pltpu
from jax.sharding import PartitionSpec as P

MESH = pl.DeviceIdType.MESH
LOW = 256
LANES = 128
TILE = 8


def parity_sign(bits):
    shift = 16
    while shift:
        bits = bits ^ (bits >> shift)
        shift //= 2
    return (1 - 2 * (bits & 1)).astype(jnp.float32)


def kernel(hi_count, lo_count, panel_hbm, signs_ref, rows_ref, picks_ref, out_ref,
           panel, field, had, sgn, terms, mine, got_a, got_b, got_c, last,
           load_sem, send_a, recv_a, send_b, recv_b, send_c, recv_c):
    count = panel.shape[0]
    blocks = count // LOW
    share = out_ref.shape[0]
    total = count * hi_count * lo_count
    side = 2 ** ((lo_count.bit_length() - 1) // 2)
    depth = lo_count // side
    plane = (hi_count // 2) * side
    hi, lo = lax.axis_index("hi"), lax.axis_index("lo")
    me = hi * lo_count + lo
    core = hi % 2
    spot = (hi // 2) * side + lo % side
    level = lo // side

    def place(core_to, level_to, spot_to):
        return ((spot_to // side) * 2 + core_to, level_to * side + spot_to % side)

    partner = place(1 - core, level, spot)
    peers_plane = [place(core, level, spot ^ j) for j in range(plane)]
    peers_depth = [place(core, level ^ r, spot) for r in range(depth)]

    loads = len(load_sem_list := [load_sem.at[i] for i in range(load_sem.shape[0])])
    rows_load = count // loads
    copies = []
    for i in range(loads):
        part = pl.ds(i * rows_load, rows_load)
        copy = pltpu.make_async_copy(panel_hbm.at[part], panel.at[part], load_sem_list[i])
        copy.start()
        copies.append(copy)

    barrier = pltpu.get_barrier_semaphore()
    greet = [partner] + peers_plane[1:] + peers_depth[1:]
    for device in greet:
        pl.semaphore_signal(barrier, inc=1, device_id=device, device_id_type=MESH)

    left = lax.broadcasted_iota(jnp.int32, (LOW, LOW), 0)
    right = lax.broadcasted_iota(jnp.int32, (LOW, LOW), 1)
    had[...] = parity_sign(left & right).astype(jnp.bfloat16)

    weight = parity_sign((picks_ref[...] // count) & me) * (1.0 / math.sqrt(total))
    for g in range(weight.shape[0]):
        sgn[pl.ds(g * LANES, LANES), :] = jnp.broadcast_to(weight[g:g + 1, :], (LANES, LANES)).T

    for i in range(loads):
        copies[i].wait()

        @pl.loop(i * (blocks // loads), (i + 1) * (blocks // loads))
        def _(a):
            for h in range(LOW // LANES):
                line = signs_ref[pl.ds(a * (LOW // LANES) + h, 1), :]
                wide = jnp.broadcast_to(line, (LANES, LANES)).T
                part = pl.ds(a * LOW + h * LANES, LANES)
                panel[part, :] = panel[part, :] * wide
            block = panel[pl.ds(a * LOW, LOW), :]
            big = block.astype(jnp.bfloat16)
            small = (block - big.astype(jnp.float32)).astype(jnp.bfloat16)
            both = jnp.concatenate([big, small], axis=1)
            done = jnp.dot(had[...], both, preferred_element_type=jnp.float32)
            field[pl.ds(a * LOW, LOW), :] = done[:, :LANES] + done[:, LANES:]

    @pl.loop(0, LOW // TILE)
    def _(p):
        parts = [field[pl.ds(b * LOW + p * TILE, TILE), :] for b in range(blocks)]
        half = 1
        while half < blocks:
            for b in range(blocks):
                if not b & half:
                    x, y = parts[b], parts[b + half]
                    parts[b], parts[b + half] = x + y, x - y
            half *= 2
        for b in range(blocks):
            field[pl.ds(b * LOW + p * TILE, TILE), :] = parts[b]

    pl.semaphore_wait(barrier, len(greet))

    def gather(dst, core_to, level_to):
        @pl.loop(0, plane)
        def _(j):
            hi_to, lo_to = place(core_to, level_to, spot ^ j)
            start = (hi_to * lo_count + lo_to) * share
            for s in range(share):
                row = rows_ref[start + s] & (count - 1)
                dst[pl.ds(j * share + s, 1), :] = field[pl.ds(row, 1), :]
            part = pl.ds(j * share, share)
            dst[part, :] = dst[part, :] * sgn[pl.ds(start, share), :]

    def remote(src, dst, send, recv, device):
        return pltpu.make_async_remote_copy(
            src_ref=src, dst_ref=dst, send_sem=send, recv_sem=recv,
            device_id=device, device_id_type=MESH)

    order = list(range(1, depth)) + [0]
    sent_b, sent_c = {}, {}

    def finish_plane(r):
        total_rows = mine[r, pl.ds(0, share), :]
        for j in range(1, plane):
            sent_b[r][j].wait_recv()
            total_rows = total_rows + got_b[r, pl.ds(j * share, share), :]
        last[r] = total_rows
        if r:
            sent_c[r] = remote(last.at[r], got_c.at[r], send_c.at[r], recv_c.at[r], peers_depth[r])
            sent_c[r].start()

    sent_a = {}
    previous = None
    for r in order:
        gather(terms.at[r], 1 - core, level ^ r)
        sent_a[r] = remote(terms.at[r], got_a.at[r], send_a.at[r], recv_a.at[r], partner)
        sent_a[r].start()
        gather(mine.at[r], core, level ^ r)
        sent_a[r].wait_recv()
        mine[r] = mine[r] + got_a[r]
        sent_b[r] = {}
        for j in range(1, plane):
            part = pl.ds(j * share, share)
            sent_b[r][j] = remote(mine.at[r, part], got_b.at[r, part],
                                  send_b.at[r, j], recv_b.at[r, j], peers_plane[j])
            sent_b[r][j].start()
        if previous is not None:
            finish_plane(previous)
        previous = r
    finish_plane(previous)
    result = last[0]
    for r in order[:-1]:
        sent_c[r].wait_recv()
        result = result + got_c[r]
    out_ref[...] = result
    for r in order:
        sent_a[r].wait_send()
        for j in range(1, plane):
            sent_b[r][j].wait_send()
        if r:
            sent_c[r].wait_send()


def body(panel, row_signs, sample_rows):
    count, width = panel.shape
    hi_count, lo_count = lax.axis_size("hi"), lax.axis_size("lo")
    kept = sample_rows.shape[0]
    share = kept // (hi_count * lo_count)
    side = 2 ** ((lo_count.bit_length() - 1) // 2)
    depth = lo_count // side
    plane = (hi_count // 2) * side
    loads = 8
    vmem = pl.BlockSpec(memory_space=pltpu.VMEM)
    dma = pltpu.SemaphoreType.DMA
    f32 = jnp.float32
    chunk = (depth, plane * share, width)
    return pl.pallas_call(
        functools.partial(kernel, hi_count, lo_count),
        out_shape=jax.ShapeDtypeStruct((share, width), f32),
        in_specs=[pl.BlockSpec(memory_space=pl.ANY), vmem,
                  pl.BlockSpec(memory_space=pltpu.SMEM), vmem],
        out_specs=vmem,
        scratch_shapes=[
            pltpu.VMEM((count, width), f32),
            pltpu.VMEM((count, width), f32),
            pltpu.VMEM((LOW, LOW), jnp.bfloat16),
            pltpu.VMEM((kept, width), f32),
            pltpu.VMEM(chunk, f32),
            pltpu.VMEM(chunk, f32),
            pltpu.VMEM(chunk, f32),
            pltpu.VMEM(chunk, f32),
            pltpu.VMEM((depth, share, width), f32),
            pltpu.VMEM((depth, share, width), f32),
            dma((loads,)),
            dma((depth,)), dma((depth,)),
            dma((depth, plane)), dma((depth, plane)),
            dma((depth,)), dma((depth,)),
        ],
        compiler_params=pltpu.CompilerParams(
            collective_id=0, has_side_effects=True, vmem_limit_bytes=40 * 2**20),
        cost_estimate=pl.CostEstimate(
            flops=2 * count * LOW * 2 * width, bytes_accessed=count * width * 4, transcendentals=0),
    )(panel, row_signs.reshape(count // LANES, LANES), sample_rows,
      sample_rows.reshape(kept // LANES, LANES))


def solution(mesh):
    placed = (P(("hi", "lo"), None), P(("hi", "lo"), None), P())
    return jax.shard_map(
        body, mesh=mesh, in_specs=placed, out_specs=P(("hi", "lo"), None), check_vma=False
    )
```

```python
import functools
import math

import jax
import jax.numpy as jnp
from jax import lax
from jax.experimental import pallas as pl
from jax.experimental.pallas import tpu as pltpu
from jax.sharding import PartitionSpec as P

MESH = pl.DeviceIdType.MESH
LOW = 256
LANES = 128
TILE = 8


def parity_sign(bits):
    shift = 16
    while shift:
        bits = bits ^ (bits >> shift)
        shift //= 2
    return (1 - 2 * (bits & 1)).astype(jnp.float32)


def kernel(hi_count, lo_count, panel_hbm, signs_hbm, rows_hbm, picks_hbm, out_ref,
           panel, signs_ref, rows_ref, picks_ref, field, had, sgn, terms, mine, got_a, got_b, got_c, last,
           load_sem, small_sem, send_a, recv_a, send_b, recv_b, send_c, recv_c):
    count = panel.shape[0]
    blocks = count // LOW
    share = out_ref.shape[0]
    total = count * hi_count * lo_count
    side = 2 ** ((lo_count.bit_length() - 1) // 2)
    depth = lo_count // side
    plane = (hi_count // 2) * side
    hi, lo = lax.axis_index("hi"), lax.axis_index("lo")
    me = hi * lo_count + lo
    core = hi % 2
    spot = (hi // 2) * side + lo % side
    level = lo // side

    def place(core_to, level_to, spot_to):
        return ((spot_to // side) * 2 + core_to, level_to * side + spot_to % side)

    partner = place(1 - core, level, spot)
    peers_plane = [place(core, level, spot ^ j) for j in range(plane)]
    peers_depth = [place(core, level ^ r, spot) for r in range(depth)]

    loads = load_sem.shape[0]
    rows_load = count // loads
    small = [pltpu.make_async_copy(signs_hbm, signs_ref, small_sem.at[0]),
             pltpu.make_async_copy(picks_hbm, picks_ref, small_sem.at[1]),
             pltpu.make_async_copy(rows_hbm, rows_ref, small_sem.at[2])]
    for copy in small:
        copy.start()

    def load(i):
        part = pl.ds(i * rows_load, rows_load)
        return pltpu.make_async_copy(panel_hbm.at[part], panel.at[part], load_sem.at[i])

    for i in range(loads):
        load(i).start()

    barrier = pltpu.get_barrier_semaphore()
    greet = [partner] + peers_plane[1:] + peers_depth[1:]
    for device in greet:
        pl.semaphore_signal(barrier, inc=1, device_id=device, device_id_type=MESH)

    left = lax.broadcasted_iota(jnp.int32, (LOW, LOW), 0)
    right = lax.broadcasted_iota(jnp.int32, (LOW, LOW), 1)
    had[...] = parity_sign(left & right).astype(jnp.bfloat16)

    for copy in small:
        copy.wait()

    weight = parity_sign((picks_ref[...] // count) & me) * (1.0 / math.sqrt(total))
    for g in range(weight.shape[0]):
        sgn[pl.ds(g * LANES, LANES), :] = jnp.broadcast_to(weight[g:g + 1, :], (LANES, LANES)).T

    @pl.loop(0, loads)
    def _(i):
        load(i).wait()
        for step in range(blocks // loads):
            a = i * (blocks // loads) + step
            parts = []
            for h in range(LOW // LANES):
                line = signs_ref[pl.ds(a * (LOW // LANES) + h, 1), :]
                wide = jnp.broadcast_to(line, (LANES, LANES)).T
                parts.append(panel[pl.ds(a * LOW + h * LANES, LANES), :] * wide)
            block = jnp.concatenate(parts, axis=0)
            big = block.astype(jnp.bfloat16)
            small = (block - big.astype(jnp.float32)).astype(jnp.bfloat16)
            both = jnp.concatenate([big, small], axis=1)
            done = jnp.dot(had[...], both, preferred_element_type=jnp.float32)
            field[pl.ds(a * LOW, LOW), :] = done[:, :LANES] + done[:, LANES:]

    @pl.loop(0, LOW // TILE)
    def _(p):
        parts = [field[pl.ds(b * LOW + p * TILE, TILE), :] for b in range(blocks)]
        half = 1
        while half < blocks:
            for b in range(blocks):
                if not b & half:
                    x, y = parts[b], parts[b + half]
                    parts[b], parts[b + half] = x + y, x - y
            half *= 2
        for b in range(blocks):
            field[pl.ds(b * LOW + p * TILE, TILE), :] = parts[b]

    pl.semaphore_wait(barrier, len(greet))

    def gather(dst, core_to, level_to):
        @pl.loop(0, plane)
        def _(j):
            hi_to, lo_to = place(core_to, level_to, spot ^ j)
            start = (hi_to * lo_count + lo_to) * share
            for s in range(share):
                row = rows_ref[start + s] & (count - 1)
                dst[pl.ds(j * share + s, 1), :] = field[pl.ds(row, 1), :]
            part = pl.ds(j * share, share)
            dst[part, :] = dst[part, :] * sgn[pl.ds(start, share), :]

    def remote(src, dst, send, recv, device):
        return pltpu.make_async_remote_copy(
            src_ref=src, dst_ref=dst, send_sem=send, recv_sem=recv,
            device_id=device, device_id_type=MESH)

    levels = range(depth)
    sent_a, sent_b = {}, {}

    def send_pair(c):
        gather(terms.at[c], 1 - core, c)
        sent_a[c] = remote(terms.at[c], got_a.at[c], send_a.at[c], recv_a.at[c], partner)
        sent_a[c].start()
        gather(mine.at[c], core, c)

    def send_plane(c):
        sent_a[c].wait_recv()
        for j in list(range(1, plane)) + [0]:
            part = pl.ds(j * share, share)
            mine[c, part, :] = mine[c, part, :] + got_a[c, part, :]
            if j:
                sent_b[c, j] = remote(mine.at[c, part], got_b.at[c, part],
                                      send_b.at[c, j], recv_b.at[c, j], peers_plane[j])
                sent_b[c, j].start()

    def to_level(c):
        return remote(last.at[c], got_c.at[level], send_c.at[c], recv_c.at[level],
                      place(core, c, spot))

    def send_level(c):
        rows = mine[c, pl.ds(0, share), :]
        for j in range(1, plane):
            sent_b[c, j].wait_recv()
            rows = rows + got_b[c, pl.ds(j * share, share), :]
        last[c] = rows

        @pl.when(level != c)
        def _():
            to_level(c).start()

    for c in levels:
        send_pair(c)
        if c:
            send_plane(c - 1)
    send_plane(depth - 1)
    for c in levels:
        send_level(c)
    result = last[level]
    for r in range(1, depth):
        other = level ^ r
        remote(last.at[other], got_c.at[other], send_c.at[other], recv_c.at[other],
               place(core, other, spot)).wait_recv()
        result = result + got_c[other]
    out_ref[...] = result
    for c in levels:
        sent_a[c].wait_send()
        for j in range(1, plane):
            sent_b[c, j].wait_send()

        @pl.when(level != c)
        def _():
            to_level(c).wait_send()


def body(panel, row_signs, sample_rows):
    count, width = panel.shape
    hi_count, lo_count = lax.axis_size("hi"), lax.axis_size("lo")
    kept = sample_rows.shape[0]
    share = kept // (hi_count * lo_count)
    side = 2 ** ((lo_count.bit_length() - 1) // 2)
    depth = lo_count // side
    plane = (hi_count // 2) * side
    loads = 2
    vmem = pl.BlockSpec(memory_space=pltpu.VMEM)
    dma = pltpu.SemaphoreType.DMA
    f32 = jnp.float32
    chunk = (depth, plane * share, width)
    return pl.pallas_call(
        functools.partial(kernel, hi_count, lo_count),
        out_shape=jax.ShapeDtypeStruct((share, width), f32),
        in_specs=[pl.BlockSpec(memory_space=pltpu.HBM)] * 4,
        out_specs=vmem,
        scratch_shapes=[
            pltpu.VMEM((count, width), f32),
            pltpu.VMEM((count // LANES, LANES), f32),
            pltpu.SMEM((kept,), jnp.int32),
            pltpu.VMEM((kept // LANES, LANES), jnp.int32),
            pltpu.VMEM((count, width), f32),
            pltpu.VMEM((LOW, LOW), jnp.bfloat16),
            pltpu.VMEM((kept, width), f32),
            pltpu.VMEM(chunk, f32),
            pltpu.VMEM(chunk, f32),
            pltpu.VMEM(chunk, f32),
            pltpu.VMEM(chunk, f32),
            pltpu.VMEM((depth, share, width), f32),
            pltpu.VMEM((depth, share, width), f32),
            dma((loads,)), dma((3,)),
            dma((depth,)), dma((depth,)),
            dma((depth, plane)), dma((depth, plane)),
            dma((depth,)), dma((depth,)),
        ],
        compiler_params=pltpu.CompilerParams(
            collective_id=0, has_side_effects=True, vmem_limit_bytes=60 * 2**20),
        cost_estimate=pl.CostEstimate(
            flops=2 * count * LOW * 2 * width, bytes_accessed=count * width * 4, transcendentals=0),
    )(panel, row_signs.reshape(count // LANES, LANES), sample_rows,
      sample_rows.reshape(kept // LANES, LANES))


def solution(mesh):
    placed = (P(("hi", "lo"), None), P(("hi", "lo"), None), P())
    return jax.shard_map(
        body, mesh=mesh, in_specs=placed, out_specs=P(("hi", "lo"), None), check_vma=False
    )
```

```python
import functools
import math

import jax
import jax.numpy as jnp
from jax import lax
from jax.experimental import pallas as pl
from jax.experimental.pallas import tpu as pltpu
from jax.sharding import PartitionSpec as P

MESH = pl.DeviceIdType.MESH
LOW = 256
LANES = 128
TILE = 8


def parity_sign(bits):
    shift = 16
    while shift:
        bits = bits ^ (bits >> shift)
        shift //= 2
    return (1 - 2 * (bits & 1)).astype(jnp.float32)


def kernel(hi_count, lo_count, panel_hbm, signs_hbm, rows_hbm, picks_hbm, out_ref,
           panel, signs_ref, rows_ref, picks_ref, field, had, sgn, terms, mine, got_a, got_b, got_c, last,
           load_sem, small_sem, send_a, recv_a, send_b, recv_b, send_c, recv_c):
    count = panel.shape[0]
    blocks = count // LOW
    share = out_ref.shape[0]
    total = count * hi_count * lo_count
    side = 2 ** ((lo_count.bit_length() - 1) // 2)
    depth = lo_count // side
    plane = (hi_count // 2) * side
    hi, lo = lax.axis_index("hi"), lax.axis_index("lo")
    me = hi * lo_count + lo
    core = hi % 2
    spot = (hi // 2) * side + lo % side
    level = lo // side

    def place(core_to, level_to, spot_to):
        return ((spot_to // side) * 2 + core_to, level_to * side + spot_to % side)

    partner = place(1 - core, level, spot)
    peers_plane = [place(core, level, spot ^ j) for j in range(plane)]
    peers_depth = [place(core, level ^ r, spot) for r in range(depth)]

    loads = load_sem.shape[0]
    rows_load = count // loads
    small = [pltpu.make_async_copy(signs_hbm, signs_ref, small_sem.at[0]),
             pltpu.make_async_copy(picks_hbm, picks_ref, small_sem.at[1]),
             pltpu.make_async_copy(rows_hbm, rows_ref, small_sem.at[2])]
    for copy in small:
        copy.start()

    def load(i):
        part = pl.ds(i * rows_load, rows_load)
        return pltpu.make_async_copy(panel_hbm.at[part], panel.at[part], load_sem.at[i])

    for i in range(loads):
        load(i).start()

    barrier = pltpu.get_barrier_semaphore()
    greet = [partner] + peers_plane[1:] + peers_depth[1:]
    for device in greet:
        pl.semaphore_signal(barrier, inc=1, device_id=device, device_id_type=MESH)

    left = lax.broadcasted_iota(jnp.int32, (LOW, LOW), 0)
    right = lax.broadcasted_iota(jnp.int32, (LOW, LOW), 1)
    had[...] = parity_sign(left & right).astype(jnp.bfloat16)

    for copy in small:
        copy.wait()

    weight = parity_sign((picks_ref[...] // count) & me) * (1.0 / math.sqrt(total))
    for g in range(weight.shape[0]):
        sgn[pl.ds(g * LANES, LANES), :] = jnp.broadcast_to(weight[g:g + 1, :], (LANES, LANES)).T

    @pl.loop(0, loads)
    def _(i):
        load(i).wait()
        for step in range(blocks // loads):
            a = i * (blocks // loads) + step
            parts = []
            for h in range(LOW // LANES):
                line = signs_ref[pl.ds(a * (LOW // LANES) + h, 1), :]
                wide = jnp.broadcast_to(line, (LANES, LANES)).T
                parts.append(panel[pl.ds(a * LOW + h * LANES, LANES), :] * wide)
            block = jnp.concatenate(parts, axis=0)
            big = block.astype(jnp.bfloat16)
            small = (block - big.astype(jnp.float32)).astype(jnp.bfloat16)
            both = jnp.concatenate([big, small], axis=1)
            done = jnp.dot(had[...], both, preferred_element_type=jnp.float32)
            field[pl.ds(a * LOW, LOW), :] = done[:, :LANES] + done[:, LANES:]

    @pl.loop(0, LOW // TILE)
    def _(p):
        parts = [field[pl.ds(b * LOW + p * TILE, TILE), :] for b in range(blocks)]
        half = 1
        while half < blocks:
            for b in range(blocks):
                if not b & half:
                    x, y = parts[b], parts[b + half]
                    parts[b], parts[b + half] = x + y, x - y
            half *= 2
        for b in range(blocks):
            field[pl.ds(b * LOW + p * TILE, TILE), :] = parts[b]

    pl.semaphore_wait(barrier, len(greet))

    def gather(dst, core_to, level_to):
        @pl.loop(0, plane)
        def _(j):
            hi_to, lo_to = place(core_to, level_to, spot ^ j)
            start = (hi_to * lo_count + lo_to) * share
            for s in range(share):
                row = rows_ref[start + s] & (count - 1)
                dst[pl.ds(j * share + s, 1), :] = field[pl.ds(row, 1), :]
            part = pl.ds(j * share, share)
            dst[part, :] = dst[part, :] * sgn[pl.ds(start, share), :]

    def remote(src, dst, send, recv, device):
        return pltpu.make_async_remote_copy(
            src_ref=src, dst_ref=dst, send_sem=send, recv_sem=recv,
            device_id=device, device_id_type=MESH)

    levels = range(depth)
    sent_a, sent_b = {}, {}

    def send_pair(c):
        gather(terms.at[c], 1 - core, c)
        sent_a[c] = remote(terms.at[c], got_a.at[c], send_a.at[c], recv_a.at[c], partner)
        sent_a[c].start()
        if c:
            send_plane(c - 1)
        gather(mine.at[c], core, c)

    def send_plane(c):
        sent_a[c].wait_recv()
        for j in list(range(1, plane)) + [0]:
            part = pl.ds(j * share, share)
            mine[c, part, :] = mine[c, part, :] + got_a[c, part, :]
            if j:
                sent_b[c, j] = remote(mine.at[c, part], got_b.at[c, part],
                                      send_b.at[c, j], recv_b.at[c, j], peers_plane[j])
                sent_b[c, j].start()

    def to_level(c):
        return remote(last.at[c], got_c.at[level], send_c.at[c], recv_c.at[level],
                      place(core, c, spot))

    def send_level(c):
        rows = mine[c, pl.ds(0, share), :]
        for j in range(1, plane):
            sent_b[c, j].wait_recv()
            rows = rows + got_b[c, pl.ds(j * share, share), :]
        last[c] = rows

        @pl.when(level != c)
        def _():
            to_level(c).start()

    for c in levels:
        send_pair(c)
    send_plane(depth - 1)
    for c in levels:
        send_level(c)
    result = last[level]
    for r in range(1, depth):
        other = level ^ r
        remote(last.at[other], got_c.at[other], send_c.at[other], recv_c.at[other],
               place(core, other, spot)).wait_recv()
        result = result + got_c[other]
    out_ref[...] = result
    for c in levels:
        sent_a[c].wait_send()
        for j in range(1, plane):
            sent_b[c, j].wait_send()

        @pl.when(level != c)
        def _():
            to_level(c).wait_send()


def body(panel, row_signs, sample_rows):
    count, width = panel.shape
    hi_count, lo_count = lax.axis_size("hi"), lax.axis_size("lo")
    kept = sample_rows.shape[0]
    share = kept // (hi_count * lo_count)
    side = 2 ** ((lo_count.bit_length() - 1) // 2)
    depth = lo_count // side
    plane = (hi_count // 2) * side
    loads = 2
    vmem = pl.BlockSpec(memory_space=pltpu.VMEM)
    dma = pltpu.SemaphoreType.DMA
    f32 = jnp.float32
    chunk = (depth, plane * share, width)
    return pl.pallas_call(
        functools.partial(kernel, hi_count, lo_count),
        out_shape=jax.ShapeDtypeStruct((share, width), f32),
        in_specs=[pl.BlockSpec(memory_space=pltpu.HBM)] * 4,
        out_specs=vmem,
        scratch_shapes=[
            pltpu.VMEM((count, width), f32),
            pltpu.VMEM((count // LANES, LANES), f32),
            pltpu.SMEM((kept,), jnp.int32),
            pltpu.VMEM((kept // LANES, LANES), jnp.int32),
            pltpu.VMEM((count, width), f32),
            pltpu.VMEM((LOW, LOW), jnp.bfloat16),
            pltpu.VMEM((kept, width), f32),
            pltpu.VMEM(chunk, f32),
            pltpu.VMEM(chunk, f32),
            pltpu.VMEM(chunk, f32),
            pltpu.VMEM(chunk, f32),
            pltpu.VMEM((depth, share, width), f32),
            pltpu.VMEM((depth, share, width), f32),
            dma((loads,)), dma((3,)),
            dma((depth,)), dma((depth,)),
            dma((depth, plane)), dma((depth, plane)),
            dma((depth,)), dma((depth,)),
        ],
        compiler_params=pltpu.CompilerParams(
            collective_id=0, has_side_effects=True, vmem_limit_bytes=60 * 2**20),
        cost_estimate=pl.CostEstimate(
            flops=2 * count * LOW * 2 * width, bytes_accessed=count * width * 4, transcendentals=0),
    )(panel, row_signs.reshape(count // LANES, LANES), sample_rows,
      sample_rows.reshape(kept // LANES, LANES))


def solution(mesh):
    placed = (P(("hi", "lo"), None), P(("hi", "lo"), None), P())
    return jax.shard_map(
        body, mesh=mesh, in_specs=placed, out_specs=P(("hi", "lo"), None), check_vma=False
    )
```
